256 devices in a mesh: tm: 32 (over y, x, core), head: 8 (over z).
Axes of the slice: x: 4, y: 4, z: 8, core: 2. Of those that a mesh axis runs over, the one named last changes fastest.
Arguments:
- queries: bfloat16 [16384, 3072], P('tm', 'head'), may hold values from -700 to 700
- key_rows: bfloat16 [16384, 3072], P('tm', 'head'), may hold values from -700 to 700
- value_rows: bfloat16 [16384, 3072], P('tm', 'head'), may hold values from -6 to 6
- query_gain: float32 [3072], P('head'), may hold values from 0.1 to 1.9
- key_gain: float32 [3072], P('head'), may hold values from 0.1 to 1.9
- block_mask: int32 [32, 7, 4, 4], replicated, may hold values from 0 to 1, as said below
- out_grad: bfloat16 [16384, 3072], P('tm', 'head'), may hold values from -6 to 6
Outputs:
- attended: bfloat16 [16384, 3072], P('tm', 'head')
- query_grad: bfloat16 [16384, 3072], P('tm', 'head')
- key_grad: bfloat16 [16384, 3072], P('tm', 'head')
- value_grad: bfloat16 [16384, 3072], P('tm', 'head')
The draws below stay inside these ranges and needn't reach their ends.
Inputs may be any that keep to these rules, and one draw needn't show every extreme that they name: block_mask[f, 3] is all ones; for every f and j some entry of block_mask[f, j] is one.
All inputs are finite; a program needn't handle non-finite values.
Results may differ from the reference program's by a relative error of at most 0.022.
Values may be sent and summed in bfloat16 or wider, within the bound.
No kernel may reach another device: no remote copies, remote signals or barrier semaphores. Data moves between devices by JAX's collectives and lax.ppermute only.
A program may use at most 128 MiB of HBM per device.

```python
import math
import jax
import jax.numpy as jnp
from jax import lax

HEADS = 24
HEAD_DIM = 128
BLK = 128
REACH = 3
FT = 512
WIDTH = 3072
NF = 32
TOKENS = 16384


def scale_tables(key, rise):
    column_key, row_key = jax.random.split(key)
    columns = jnp.arange(WIDTH, dtype=jnp.float32) / WIDTH
    column_scale = jnp.exp(jax.random.uniform(column_key, (WIDTH,), jnp.float32) * math.log(10.0)) * rise ** (0.5 * columns)
    row_scale = jnp.exp(jax.random.uniform(row_key, (TOKENS, 1), jnp.float32) * math.log(10.0))
    return (column_scale, row_scale)


def draw_queries(key, part):
    key = jax.random.fold_in(key, 3)
    base_key, scale_key = jax.random.split(key)
    base_draw = jnp.clip(jax.random.normal(base_key, (TOKENS, WIDTH), jnp.float32), -4.0, 4.0)
    column_scale, row_scale = scale_tables(scale_key, 3.0)
    result = base_draw * row_scale * column_scale
    return result.astype(jnp.bfloat16)


def draw_key_rows(key, part):
    key = jax.random.fold_in(key, 5)
    base_key, scale_key = jax.random.split(key)
    base_draw = jnp.clip(jax.random.normal(base_key, (TOKENS, WIDTH), jnp.float32), -4.0, 4.0)
    column_scale, row_scale = scale_tables(scale_key, 3.0)
    result = base_draw * row_scale * column_scale
    return result.astype(jnp.bfloat16)


def draw_block_mask(key, part):
    key = jax.random.fold_in(key, 7)
    lottery_key, forced_key = jax.random.split(key)
    blocks = FT // BLK
    band_size = 2 * REACH + 1
    distance = jnp.abs(jnp.arange(band_size, dtype=jnp.int32) - REACH)[None, :, None, None]
    lottery = jax.random.randint(lottery_key, (NF, band_size, blocks, blocks), 0, 840, jnp.int32)
    forced = jax.random.randint(forced_key, (NF, band_size, 1, 1), 0, blocks * blocks, jnp.int32)
    position = jnp.arange(blocks, dtype=jnp.int32)[:, None] * blocks + jnp.arange(blocks, dtype=jnp.int32)[None, :]
    is_live = (lottery % (distance + 1) == 0) | (position[None, None] == forced) | (distance == 0)
    return is_live.astype(jnp.int32)


def block_scale(own_key, shape, cuts, low, top_value):
    loudness = 1.0
    for dim, blocks in cuts:
        steps = jax.random.uniform(jax.random.fold_in(jax.random.fold_in(own_key, 6), dim), (blocks,), jnp.float32, low / len(cuts), top_value / len(cuts))
        loudness = loudness * jnp.repeat(jnp.exp(steps), shape[dim] // blocks).reshape((-1,) + (1,) * (len(shape) - 1 - dim))
    return loudness


def noise(rng, dims, spread, reach, pieces=(), kind=jnp.bfloat16):
    drawn = spread * jax.random.normal(rng, dims, jnp.float32)
    if pieces:
        drawn = drawn * block_scale(rng, dims, pieces, -0.22, 0.18)
    return jnp.clip(drawn, -reach, reach).astype(kind)


def setup_inputs(seed: int = 0) -> dict:
    arg_keys = jax.random.split(jax.random.key(seed), 8)
    queries = draw_queries(jax.random.fold_in(arg_keys[7], 71), 0)
    key_rows = draw_key_rows(jax.random.fold_in(arg_keys[7], 71), 0)
    value_rows = noise(arg_keys[2], (TOKENS, WIDTH), 1.0, 6.0, ((0, 32), (1, 8)))
    query_gain = jnp.clip(1.0 + 0.18 * jax.random.normal(arg_keys[3], (WIDTH,), jnp.float32), 0.1, 1.9)
    key_gain = jnp.clip(1.0 + 0.18 * jax.random.normal(arg_keys[4], (WIDTH,), jnp.float32), 0.1, 1.9)
    block_mask = draw_block_mask(jax.random.fold_in(arg_keys[7], 71), 0)
    out_grad = noise(arg_keys[6], (TOKENS, WIDTH), 1.0, 6.0, ((0, 32), (1, 8)))
    return {"queries": queries, "key_rows": key_rows, "value_rows": value_rows, "query_gain": query_gain, "key_gain": key_gain, "block_mask": block_mask, "out_grad": out_grad}


def normalized(raw, gain):
    as_float = raw.astype(jnp.float32)
    rate = lax.rsqrt(lax.optimization_barrier(jnp.sum(as_float * as_float, axis=1, keepdims=True)) / WIDTH + 1e-06)
    return (as_float, rate, (as_float * rate * gain).astype(jnp.bfloat16))

def expand_live(mask_rows, is_valid):
    band_size = mask_rows.shape[0]
    blocks = mask_rows.shape[1]
    live_blocks = (mask_rows > 0) & is_valid[:, None, None]
    expanded = jnp.broadcast_to(live_blocks[:, :, None, :, None], (band_size, blocks, BLK, blocks, BLK))
    expanded = expanded.reshape(band_size, blocks * BLK, blocks * BLK)
    return jnp.transpose(expanded, (1, 0, 2)).reshape(blocks * BLK, band_size * blocks * BLK)

def reference(queries, key_rows, value_rows, query_gain, key_gain, block_mask, out_grad):
    band_size = 2 * REACH + 1
    score_scale = HEAD_DIM ** (-0.5)
    query_float, query_rate, query_norm = normalized(queries, query_gain)
    key_float, key_rate, key_norm = normalized(key_rows, key_gain)
    padding = ((REACH, REACH), (0, 0), (0, 0))
    key_padded = jnp.pad(key_norm.reshape(NF, FT, WIDTH), padding)
    value_padded = jnp.pad(value_rows.reshape(NF, FT, WIDTH), padding)
    query_frames = query_norm.reshape(NF, FT, HEADS, HEAD_DIM)
    grad_frames = out_grad.reshape(NF, FT, HEADS, HEAD_DIM)
    offsets = jnp.arange(band_size, dtype=jnp.int32) - REACH

    def frame_step(buffers, frame_index):
        grad_keys, grad_values = buffers
        key_band = lax.dynamic_slice_in_dim(key_padded, frame_index, band_size, 0)
        key_band = key_band.reshape(band_size * FT, HEADS, HEAD_DIM).astype(jnp.float32)
        value_band = lax.dynamic_slice_in_dim(value_padded, frame_index, band_size, 0)
        value_band = value_band.reshape(band_size * FT, HEADS, HEAD_DIM).astype(jnp.float32)
        query_here = lax.dynamic_index_in_dim(query_frames, frame_index, 0, keepdims=False).astype(jnp.float32)
        grad_here = lax.dynamic_index_in_dim(grad_frames, frame_index, 0, keepdims=False).astype(jnp.float32)
        mask_rows = lax.dynamic_index_in_dim(block_mask, frame_index, 0, keepdims=False)
        is_valid = (frame_index + offsets >= 0) & (frame_index + offsets < NF)
        live_mask = expand_live(mask_rows, is_valid)
        scores = jnp.einsum('qhd,khd->hqk', query_here, key_band) * score_scale
        scores = jnp.where(live_mask[None], scores, -jnp.inf)
        row_top = lax.optimization_barrier(jnp.max(scores, axis=2, keepdims=True))
        log_total = row_top + jnp.log(lax.optimization_barrier(jnp.sum(jnp.exp(scores - row_top), axis=2, keepdims=True)))
        weights = jnp.exp(scores - log_total)
        weights_low = lax.optimization_barrier(weights.astype(jnp.bfloat16)).astype(jnp.float32)
        attended = jnp.einsum('hqk,khd->qhd', weights_low, value_band).astype(jnp.bfloat16)
        row_delta = jnp.einsum('qhd,qhd->hq', grad_here, attended.astype(jnp.float32))[:, :, None]
        grad_weights = jnp.einsum('qhd,khd->hqk', grad_here, value_band)
        grad_scores = (score_scale * weights * (grad_weights - row_delta)).astype(jnp.bfloat16)
        grad_scores = lax.optimization_barrier(grad_scores).astype(jnp.float32)
        grad_query = jnp.einsum('hqk,khd->qhd', grad_scores, key_band)
        grad_key = jnp.einsum('hqk,qhd->khd', grad_scores, query_here).reshape(band_size, FT, WIDTH)
        grad_value = jnp.einsum('hqk,qhd->khd', weights_low, grad_here).reshape(band_size, FT, WIDTH)
        grad_key = lax.optimization_barrier(grad_key.astype(jnp.bfloat16)).astype(jnp.float32)
        grad_value = lax.optimization_barrier(grad_value.astype(jnp.bfloat16)).astype(jnp.float32)
        current = lax.dynamic_slice_in_dim(grad_keys, frame_index, band_size, 0)
        grad_keys = lax.dynamic_update_slice_in_dim(grad_keys, current + grad_key, frame_index, 0)
        current = lax.dynamic_slice_in_dim(grad_values, frame_index, band_size, 0)
        grad_values = lax.dynamic_update_slice_in_dim(grad_values, current + grad_value, frame_index, 0)
        return ((grad_keys, grad_values), (attended.reshape(FT, WIDTH), grad_query.reshape(FT, WIDTH)))
    empty = jnp.zeros((NF + 2 * REACH, FT, WIDTH), jnp.float32)
    (grad_keys, grad_values), (attended, grad_qnorm) = lax.scan(frame_step, (empty, empty), jnp.arange(NF, dtype=jnp.int32))
    attended = attended.reshape(TOKENS, WIDTH)
    grad_qnorm = grad_qnorm.reshape(TOKENS, WIDTH)
    grad_knorm = grad_keys[REACH:REACH + NF].reshape(TOKENS, WIDTH)
    value_grad = grad_values[REACH:REACH + NF].reshape(TOKENS, WIDTH).astype(jnp.bfloat16)
    query_dot = lax.optimization_barrier(jnp.sum(query_float * query_gain * grad_qnorm, axis=1, keepdims=True))
    key_dot = lax.optimization_barrier(jnp.sum(key_float * key_gain * grad_knorm, axis=1, keepdims=True))
    query_grad = query_rate * query_gain * grad_qnorm - query_float * query_rate ** 3 * query_dot / WIDTH
    key_grad = key_rate * key_gain * grad_knorm - key_float * key_rate ** 3 * key_dot / WIDTH
    return (attended, query_grad.astype(jnp.bfloat16), key_grad.astype(jnp.bfloat16), value_grad)
```

```python
import functools
import jax, jax.numpy as jnp
from jax import lax
from jax.sharding import PartitionSpec as P
from jax.experimental import pallas as pl
from jax.experimental.pallas import tpu as pltpu

LOG2E = 1.4426950408889634
LN2 = 0.6931471805599453
SCALE = 128 ** -0.5
NEG = -1e30
BLK = 128
FT = 512
SLOTS = 7
KEYS = SLOTS * FT


def head_kernel(bias_ref, rate_ref, gain_ref, *refs):
    key_refs = refs[:SLOTS]
    value_refs = refs[SLOTS:2 * SLOTS]
    q_ref, g_ref, att_ref, gq_ref = refs[2 * SLOTS:2 * SLOTS + 4]
    term_refs = refs[2 * SLOTS + 4:4 * SLOTS + 4]
    kb, kt, vb, st = refs[4 * SLOTS + 4:]
    f32, bf = jnp.float32, jnp.bfloat16
    q = q_ref[...]
    g = g_ref[...]
    qt = q.T
    gt = g.T

    def fold(x, op):
        return op(x.reshape(-1, 8, FT), axis=0)

    m8 = jnp.full((8, FT), NEG, f32)
    for s in range(SLOTS):
        cols = slice(s * FT, (s + 1) * FT)
        normed = (key_refs[s][...].T.astype(f32) * rate_ref[s:s + 1, :] * gain_ref[...]).astype(bf)
        kb[cols, :] = normed.T
        vb[cols, :] = value_refs[s][...]
    for lo, hi in [(0, 2), (2, 4), (4, 6), (6, 7)]:
        cols = slice(lo * FT, hi * FT)
        x = jnp.dot(kb[cols, :], qt, preferred_element_type=f32)
        for b in range(4 * (hi - lo)):
            y = x[b * BLK:(b + 1) * BLK] + bias_ref[4 * lo + b:4 * lo + b + 1, :]
            st[lo * FT + b * BLK:lo * FT + (b + 1) * BLK, :] = y
            m8 = jnp.maximum(m8, fold(y, jnp.max))
    top = jnp.max(m8, axis=0, keepdims=True)

    l8 = jnp.zeros((8, FT), f32)
    ot = jnp.zeros((BLK, FT), f32)
    for lo, hi in [(0, 2), (2, 4), (4, 6), (6, 7)]:
        cols = slice(lo * FT, hi * FT)
        e = jnp.exp2(st[cols, :] - top)
        l8 = l8 + fold(e, jnp.sum)
        ot = ot + lax.dot_general(vb[cols, :], e.astype(bf), (((0,), (0,)), ((), ())), preferred_element_type=f32)
    total = jnp.sum(l8, axis=0, keepdims=True)
    lse = top + jnp.log2(total)
    att = (ot / total).astype(bf)
    delta = jnp.sum(gt.astype(f32) * att.astype(f32), axis=0, keepdims=True)
    att_ref[...] = att.T

    dqt = jnp.zeros((BLK, FT), f32)
    for lo, hi in [(0, 2), (2, 4), (4, 6), (6, 7)]:
        cols = slice(lo * FT, hi * FT)
        w = jnp.exp2(st[cols, :] - lse)
        gw = jnp.dot(vb[cols, :], gt, preferred_element_type=f32)
        ds = (w * (gw - delta)).astype(bf)
        dqt = dqt + lax.dot_general(kb[cols, :], ds, (((0,), (0,)), ((), ())), preferred_element_type=f32)
        dk = (jnp.dot(ds, q, preferred_element_type=f32) * LN2).astype(bf)
        dv = jnp.dot(w.astype(bf), g, preferred_element_type=f32).astype(bf)
        for s in range(lo, hi):
            part = slice((s - lo) * FT, (s - lo + 1) * FT)
            term_refs[s][...] = dk[part]
            term_refs[SLOTS + s][...] = dv[part]
    gq_ref[...] = dqt.T * SCALE


def square_kernel(*refs):
    out_ref = refs[-1]
    ones = jnp.ones((8, refs[0].shape[1]), jnp.bfloat16)
    contract = (((1,), (1,)), ((), ()))
    for i, ref in enumerate(refs[:-1]):
        x = ref[...].astype(jnp.float32)
        square = x * x
        high = square.astype(jnp.bfloat16)
        low = (square - high.astype(jnp.float32)).astype(jnp.bfloat16)
        total = lax.dot_general(ones, high, contract, preferred_element_type=jnp.float32)
        total = total + lax.dot_general(ones, low, contract, preferred_element_type=jnp.float32)
        out_ref[i:i + 1, :] = total[0:1, :]


def square_call(parts):
    return pl.pallas_call(
        square_kernel,
        out_shape=jax.ShapeDtypeStruct((len(parts), FT), jnp.float32),
        compiler_params=pltpu.CompilerParams(vmem_limit_bytes=32 * 1024 * 1024),
        name="row_squares",
        cost_estimate=pl.CostEstimate(flops=10**9, bytes_accessed=4 * 10**6, transcendentals=0),
    )(*parts)


def head_call(bias, rates, gain, keys, values, query, grad):
    vm = pltpu.VMEM
    bf, f32 = jnp.bfloat16, jnp.float32
    width = query.shape[1]
    rows = pl.BlockSpec((FT, BLK), lambda i: (0, i))
    return pl.pallas_call(
        head_kernel,
        grid=(width // BLK,),
        in_specs=[
            pl.BlockSpec((4 * SLOTS, FT), lambda i: (0, 0)),
            pl.BlockSpec((8, FT), lambda i: (0, 0)),
            pl.BlockSpec((BLK, 1), lambda i: (i, 0)),
        ]
        + [rows] * (2 * SLOTS + 2),
        out_specs=[rows] * (2 + 2 * SLOTS),
        out_shape=[jax.ShapeDtypeStruct((FT, width), bf), jax.ShapeDtypeStruct((FT, width), f32)]
        + [jax.ShapeDtypeStruct((FT, width), bf)] * (2 * SLOTS),
        scratch_shapes=[
            vm((KEYS, BLK), bf),
            vm((BLK, KEYS), bf),
            vm((KEYS, BLK), bf),
            vm((KEYS, FT), f32),
        ],
        compiler_params=pltpu.CompilerParams(vmem_limit_bytes=56 * 1024 * 1024),
        name="head_attention",
        cost_estimate=pl.CostEstimate(flops=9 * 10**9, bytes_accessed=12 * 10**6, transcendentals=12 * 10**6),
    )(bias, rates, gain, *keys, *values, query, grad)


epsilon = 1e-06


def shifted(value, steps):
    count = lax.axis_size("tm")
    return lax.ppermute(value, "tm", [(s, s + steps) for s in range(max(0, -steps), min(count, count - steps))])


def turned(value, steps):
    count = lax.axis_size("head")
    return lax.ppermute(value, "head", [(s, (s + steps) % count) for s in range(count)])


def ring_sum(value):
    after, before = turned(value, -1), turned(value, 1)
    pair = value + after
    return pair + before + turned(pair + before, -3) + turned(pair, 3)


def swapped(value):
    return lax.ppermute(value, "tm", [(s, s ^ 1) for s in range(lax.axis_size("tm"))])


def outward(value, steps):
    count = lax.axis_size("tm")
    pairs = [(s, s + steps) if s % 2 else (s, s - steps) for s in range(count)]
    return lax.ppermute(value, "tm", [(a, b) for a, b in pairs if 0 <= b < count])


def band(value, odd):
    ahead, behind = shifted(value, -2), shifted(value, 2)
    beside = swapped(value)
    outer = outward(jnp.where(odd, behind, ahead), 1)
    return [value, ahead, behind, beside, swapped(ahead), swapped(behind), outer]


def returned(terms):
    f32 = jnp.float32
    outer = outward(terms[6], 3)
    ahead = (terms[1].astype(f32) + swapped(terms[4]).astype(f32)).astype(jnp.bfloat16)
    behind = (terms[2].astype(f32) + swapped(terms[5]).astype(f32)).astype(jnp.bfloat16)
    beside = swapped(terms[3])
    return [terms[0], beside, outer, shifted(ahead, 2), shifted(behind, -2)]


def summed(parts):
    total = parts[0].astype(jnp.float32)
    for part in parts[1:]:
        total = total + part.astype(jnp.float32)
    return total


def local(queries, key_rows, value_rows, query_gain, key_gain, block_mask, out_grad):
    frame = lax.axis_index("tm")
    frame_count = lax.axis_size("tm")
    odd = frame % 2 == 1
    full_width = queries.shape[1] * lax.axis_size("head")
    keys = band(key_rows, odd)
    values = band(value_rows, odd)

    offsets = jnp.where(odd, jnp.array([0, 2, -2, -1, 1, -3, 3]), jnp.array([0, 2, -2, 1, 3, -1, -3]))
    mask_rows = lax.dynamic_index_in_dim(block_mask, frame, 0, keepdims=False)
    is_valid = (frame + offsets >= 0) & (frame + offsets < frame_count)
    live = jnp.where(is_valid[:, None, None], mask_rows[offsets + 3], 0)
    bias = jnp.where(jnp.swapaxes(live, 1, 2) > 0, 0.0, NEG).reshape(SLOTS * live.shape[2], live.shape[1])
    bias = jnp.repeat(bias, BLK, axis=1)

    query_float = queries.astype(jnp.float32)
    key_float = key_rows.astype(jnp.float32)
    rates = lax.rsqrt(ring_sum(square_call(keys + [queries])) / full_width + epsilon)
    query_rate = rates[SLOTS][:, None]
    key_rate = rates[0][:, None]
    query_scaled = (query_float * query_rate * query_gain * (SCALE * LOG2E)).astype(jnp.bfloat16)

    out = head_call(bias, rates, key_gain[:, None], keys, values, query_scaled, out_grad)
    attended, grad_qnorm = out[:2]
    key_parts = returned(out[2:2 + SLOTS])
    value_parts = returned(out[2 + SLOTS:])
    grad_knorm = summed(key_parts)
    value_sum = summed(value_parts)
    dots = jnp.stack(
        [
            jnp.sum(query_float * query_gain * grad_qnorm, axis=1),
            jnp.sum(key_float * key_gain * grad_knorm, axis=1),
        ]
    )
    query_dot, key_dot = ring_sum(dots)
    query_grad = (
        query_rate * query_gain * grad_qnorm
        - query_float * query_rate**3 * query_dot[:, None] / full_width
    )
    key_grad = (
        key_rate * key_gain * grad_knorm - key_float * key_rate**3 * key_dot[:, None] / full_width
    )
    return (
        attended,
        query_grad.astype(jnp.bfloat16),
        key_grad.astype(jnp.bfloat16),
        value_sum.astype(jnp.bfloat16),
    )


def solution(mesh):
    return jax.shard_map(
        local,
        mesh=mesh,
        in_specs=(
            P("tm", "head"),
            P("tm", "head"),
            P("tm", "head"),
            P("head"),
            P("head"),
            P(),
            P("tm", "head"),
        ),
        out_specs=(P("tm", "head"), P("tm", "head"), P("tm", "head"), P("tm", "head")),
        check_vma=False,
    )
```

```python
import functools
import jax, jax.numpy as jnp
from jax import lax
from jax.sharding import PartitionSpec as P
from jax.experimental import pallas as pl
from jax.experimental.pallas import tpu as pltpu

LOG2E = 1.4426950408889634
LN2 = 0.6931471805599453
SCALE = 128 ** -0.5
NEG = -1e30
BLK = 128
FT = 512
SLOTS = 7
KEYS = SLOTS * FT


def head_kernel(bias_ref, *refs):
    key_refs = refs[:SLOTS]
    value_refs = refs[SLOTS:2 * SLOTS]
    q_ref, g_ref, att_ref, gq_ref = refs[2 * SLOTS:2 * SLOTS + 4]
    term_refs = refs[2 * SLOTS + 4:4 * SLOTS + 4]
    kb, vb, st = refs[4 * SLOTS + 4:]
    f32, bf = jnp.float32, jnp.bfloat16
    q = q_ref[...]
    g = g_ref[...]
    qt = q.T
    gt = g.T

    def fold(x, op):
        return op(x.reshape(-1, 8, FT), axis=0)

    m8 = jnp.full((8, FT), NEG, f32)
    for s in range(SLOTS):
        cols = slice(s * FT, (s + 1) * FT)
        kb[cols, :] = key_refs[s][...]
        vb[cols, :] = value_refs[s][...]
    for lo, hi in [(0, 2), (2, 4), (4, 6), (6, 7)]:
        cols = slice(lo * FT, hi * FT)
        x = jnp.dot(kb[cols, :], qt, preferred_element_type=f32)
        for b in range(4 * (hi - lo)):
            y = x[b * BLK:(b + 1) * BLK] + bias_ref[4 * lo + b:4 * lo + b + 1, :]
            st[lo * FT + b * BLK:lo * FT + (b + 1) * BLK, :] = y
            m8 = jnp.maximum(m8, fold(y, jnp.max))
    top = jnp.max(m8, axis=0, keepdims=True)

    l8 = jnp.zeros((8, FT), f32)
    ot = jnp.zeros((BLK, FT), f32)
    for lo, hi in [(0, 2), (2, 4), (4, 6), (6, 7)]:
        cols = slice(lo * FT, hi * FT)
        e = jnp.exp2(st[cols, :] - top)
        l8 = l8 + fold(e, jnp.sum)
        ot = ot + lax.dot_general(vb[cols, :], e.astype(bf), (((0,), (0,)), ((), ())), preferred_element_type=f32)
    total = jnp.sum(l8, axis=0, keepdims=True)
    lse = top + jnp.log2(total)
    att = (ot / total).astype(bf)
    delta = jnp.sum(gt.astype(f32) * att.astype(f32), axis=0, keepdims=True)
    att_ref[...] = att.T

    dqt = jnp.zeros((BLK, FT), f32)
    for lo, hi in [(0, 2), (2, 4), (4, 6), (6, 7)]:
        cols = slice(lo * FT, hi * FT)
        w = jnp.exp2(st[cols, :] - lse)
        gw = jnp.dot(vb[cols, :], gt, preferred_element_type=f32)
        ds = (w * (gw - delta)).astype(bf)
        dqt = dqt + lax.dot_general(kb[cols, :], ds, (((0,), (0,)), ((), ())), preferred_element_type=f32)
        dk = (jnp.dot(ds, q, preferred_element_type=f32) * LN2).astype(bf)
        dv = jnp.dot(w.astype(bf), g, preferred_element_type=f32).astype(bf)
        for s in range(lo, hi):
            part = slice((s - lo) * FT, (s - lo + 1) * FT)
            term_refs[s][...] = dk[part]
            term_refs[SLOTS + s][...] = dv[part]
    gq_ref[...] = dqt.T * SCALE


def square_kernel(*refs):
    out_ref = refs[-1]
    ones = jnp.ones((8, refs[0].shape[1]), jnp.bfloat16)
    contract = (((1,), (1,)), ((), ()))
    for i, ref in enumerate(refs[:-1]):
        x = ref[...].astype(jnp.float32)
        square = x * x
        high = square.astype(jnp.bfloat16)
        low = (square - high.astype(jnp.float32)).astype(jnp.bfloat16)
        total = lax.dot_general(ones, high, contract, preferred_element_type=jnp.float32)
        total = total + lax.dot_general(ones, low, contract, preferred_element_type=jnp.float32)
        out_ref[i:i + 1, :] = total[0:1, :]


def square_call(parts):
    return pl.pallas_call(
        square_kernel,
        out_shape=jax.ShapeDtypeStruct((len(parts), FT), jnp.float32),
        compiler_params=pltpu.CompilerParams(vmem_limit_bytes=32 * 1024 * 1024),
        name="row_squares",
        cost_estimate=pl.CostEstimate(flops=10**9, bytes_accessed=4 * 10**6, transcendentals=0),
    )(*parts)


def head_call(bias, keys, values, query, grad):
    vm = pltpu.VMEM
    bf, f32 = jnp.bfloat16, jnp.float32
    width = query.shape[1]
    rows = pl.BlockSpec((FT, BLK), lambda i: (0, i))
    return pl.pallas_call(
        head_kernel,
        grid=(width // BLK,),
        in_specs=[
            pl.BlockSpec((4 * SLOTS, FT), lambda i: (0, 0)),
        ]
        + [rows] * (2 * SLOTS + 2),
        out_specs=[rows] * (2 + 2 * SLOTS),
        out_shape=[jax.ShapeDtypeStruct((FT, width), bf), jax.ShapeDtypeStruct((FT, width), f32)]
        + [jax.ShapeDtypeStruct((FT, width), bf)] * (2 * SLOTS),
        scratch_shapes=[
            vm((KEYS, BLK), bf),
            vm((KEYS, BLK), bf),
            vm((KEYS, FT), f32),
        ],
        compiler_params=pltpu.CompilerParams(vmem_limit_bytes=56 * 1024 * 1024),
        name="head_attention",
        cost_estimate=pl.CostEstimate(flops=9 * 10**9, bytes_accessed=12 * 10**6, transcendentals=12 * 10**6),
    )(bias, *keys, *values, query, grad)


epsilon = 1e-06


def across(value, late):
    count = lax.axis_size("tm")
    pairs = [(s, s ^ 2) if not late else (s, ((s + 2) ^ 2) - 2) for s in range(count)]
    return lax.ppermute(value, "tm", [(a, b) for a, b in pairs if 0 <= b < count])


def turned(value, steps):
    count = lax.axis_size("head")
    return lax.ppermute(value, "head", [(s, (s + steps) % count) for s in range(count)])


def ring_sum(value):
    after, before = turned(value, -1), turned(value, 1)
    pair = value + after
    return pair + before + turned(pair + before, -3) + turned(pair, 3)


def swapped(value):
    return lax.ppermute(value, "tm", [(s, s ^ 1) for s in range(lax.axis_size("tm"))])


def outward(value):
    count = lax.axis_size("tm")
    pairs = [(s, s + 1) if s % 2 else (s, s - 1) for s in range(count)]
    return lax.ppermute(value, "tm", [(a, b) for a, b in pairs if 0 <= b < count])


def band(value, cross):
    early, late = across(value, False), across(value, True)
    beside = swapped(value)
    outer = outward(jnp.where(cross, early, late))
    return [value, early, late, beside, swapped(early), swapped(late), outer]


def paired(terms, cross):
    f32 = jnp.float32
    outer = outward(terms[6]).astype(f32)
    early = terms[1].astype(f32) + swapped(terms[4]).astype(f32) + jnp.where(cross, outer, 0.0)
    late = terms[2].astype(f32) + swapped(terms[5]).astype(f32) + jnp.where(cross, 0.0, outer)
    return early.astype(jnp.bfloat16), late.astype(jnp.bfloat16)


def returned(terms, early, late):
    return [terms[0], swapped(terms[3]), across(early, False), across(late, True)]


def summed(parts):
    total = parts[0].astype(jnp.float32)
    for part in parts[1:]:
        total = total + part.astype(jnp.float32)
    return total


def local(queries, key_rows, value_rows, query_gain, key_gain, block_mask, out_grad):
    frame = lax.axis_index("tm")
    frame_count = lax.axis_size("tm")
    core = 1 - 2 * (frame % 2)
    chip = 2 - 4 * (frame // 2 % 2)
    cross = core * chip > 0
    full_width = queries.shape[1] * lax.axis_size("head")
    values = band(value_rows, cross)

    offsets = jnp.stack([0 * core, chip, -chip, core, core + chip, core - chip, -3 * core])
    mask_rows = lax.dynamic_index_in_dim(block_mask, frame, 0, keepdims=False)
    is_valid = (frame + offsets >= 0) & (frame + offsets < frame_count)
    live = jnp.where(is_valid[:, None, None], mask_rows[offsets + 3], 0)
    bias = jnp.where(jnp.swapaxes(live, 1, 2) > 0, 0.0, NEG).reshape(SLOTS * live.shape[2], live.shape[1])
    bias = jnp.repeat(bias, BLK, axis=1)

    query_float = queries.astype(jnp.float32)
    key_float = key_rows.astype(jnp.float32)
    key_raw, values[3] = lax.optimization_barrier((key_rows, values[3]))
    rates = lax.rsqrt(ring_sum(square_call([queries, key_raw])) / full_width + epsilon)
    query_rate = rates[0][:, None]
    key_rate = rates[1][:, None]
    query_scaled = (query_float * query_rate * query_gain * (SCALE * LOG2E)).astype(jnp.bfloat16)
    keys = band((key_float * key_rate * key_gain).astype(jnp.bfloat16), cross)

    out = head_call(bias, keys, values, query_scaled, out_grad)
    attended, grad_qnorm = out[:2]
    key_terms, value_terms = out[2:2 + SLOTS], out[2 + SLOTS:]
    key_parts = returned(key_terms, *paired(key_terms, cross))
    value_near = paired(value_terms, cross)
    key_parts, value_near = lax.optimization_barrier((key_parts, value_near))
    value_parts = returned(value_terms, *value_near)
    grad_knorm = summed(key_parts)
    dots = jnp.stack(
        [
            jnp.sum(query_float * query_gain * grad_qnorm, axis=1),
            jnp.sum(key_float * key_gain * grad_knorm, axis=1),
        ]
    )
    dots, value_parts = lax.optimization_barrier((ring_sum(dots), value_parts))
    query_dot, key_dot = dots
    value_sum = summed(value_parts)
    query_grad = (
        query_rate * query_gain * grad_qnorm
        - query_float * query_rate**3 * query_dot[:, None] / full_width
    )
    key_grad = (
        key_rate * key_gain * grad_knorm - key_float * key_rate**3 * key_dot[:, None] / full_width
    )
    return (
        attended,
        query_grad.astype(jnp.bfloat16),
        key_grad.astype(jnp.bfloat16),
        value_sum.astype(jnp.bfloat16),
    )


def solution(mesh):
    return jax.shard_map(
        local,
        mesh=mesh,
        in_specs=(
            P("tm", "head"),
            P("tm", "head"),
            P("tm", "head"),
            P("head"),
            P("head"),
            P(),
            P("tm", "head"),
        ),
        out_specs=(P("tm", "head"), P("tm", "head"), P("tm", "head"), P("tm", "head")),
        check_vma=False,
    )
```

```python
import functools
import jax, jax.numpy as jnp
from jax import lax
from jax.sharding import PartitionSpec as P
from jax.experimental import pallas as pl
from jax.experimental.pallas import tpu as pltpu

LOG2E = 1.4426950408889634
LN2 = 0.6931471805599453
SCALE = 128 ** -0.5
NEG = -1e30
BLK = 128
FT = 512
SLOTS = 7
KEYS = SLOTS * FT


def head_kernel(bias_ref, *refs):
    key_refs = refs[:SLOTS]
    value_refs = refs[SLOTS:2 * SLOTS]
    q_ref, g_ref, att_ref, gq_ref = refs[2 * SLOTS:2 * SLOTS + 4]
    term_refs = refs[2 * SLOTS + 4:4 * SLOTS + 4]
    kb, vb, st = refs[4 * SLOTS + 4:]
    f32, bf = jnp.float32, jnp.bfloat16
    q = q_ref[...]
    g = g_ref[...]
    qt = q.T
    gt = g.T

    def fold(x, op):
        return op(x.reshape(-1, 8, FT), axis=0)

    m8 = jnp.full((8, FT), NEG, f32)
    for s in range(SLOTS):
        cols = slice(s * FT, (s + 1) * FT)
        kb[cols, :] = key_refs[s][...]
        vb[cols, :] = value_refs[s][...]
    for lo, hi in [(0, 2), (2, 4), (4, 6), (6, 7)]:
        cols = slice(lo * FT, hi * FT)
        x = jnp.dot(kb[cols, :], qt, preferred_element_type=f32)
        for b in range(4 * (hi - lo)):
            y = x[b * BLK:(b + 1) * BLK] + bias_ref[4 * lo + b:4 * lo + b + 1, :]
            st[lo * FT + b * BLK:lo * FT + (b + 1) * BLK, :] = y
            m8 = jnp.maximum(m8, fold(y, jnp.max))
    top = jnp.max(m8, axis=0, keepdims=True)

    l8 = jnp.zeros((8, FT), f32)
    ot = jnp.zeros((BLK, FT), f32)
    for lo, hi in [(0, 2), (2, 4), (4, 6), (6, 7)]:
        cols = slice(lo * FT, hi * FT)
        e = jnp.exp2(st[cols, :] - top)
        l8 = l8 + fold(e, jnp.sum)
        ot = ot + lax.dot_general(vb[cols, :], e.astype(bf), (((0,), (0,)), ((), ())), preferred_element_type=f32)
    total = jnp.sum(l8, axis=0, keepdims=True)
    lse = top + jnp.log2(total)
    att = (ot / total).astype(bf)
    delta = jnp.sum(gt.astype(f32) * att.astype(f32), axis=0, keepdims=True)
    att_ref[...] = att.T

    dqt = jnp.zeros((BLK, FT), f32)
    for lo, hi in [(0, 2), (2, 4), (4, 6), (6, 7)]:
        cols = slice(lo * FT, hi * FT)
        w = jnp.exp2(st[cols, :] - lse)
        gw = jnp.dot(vb[cols, :], gt, preferred_element_type=f32)
        ds = (w * (gw - delta)).astype(bf)
        dqt = dqt + lax.dot_general(kb[cols, :], ds, (((0,), (0,)), ((), ())), preferred_element_type=f32)
        dk = (jnp.dot(ds, q, preferred_element_type=f32) * LN2).astype(bf)
        dv = jnp.dot(w.astype(bf), g, preferred_element_type=f32).astype(bf)
        for s in range(lo, hi):
            part = slice((s - lo) * FT, (s - lo + 1) * FT)
            term_refs[s][...] = dk[part]
            term_refs[SLOTS + s][...] = dv[part]
    gq_ref[...] = dqt.T * SCALE


def square_kernel(*refs):
    out_ref = refs[-1]
    ones = jnp.ones((8, refs[0].shape[1]), jnp.bfloat16)
    contract = (((1,), (1,)), ((), ()))
    for i, ref in enumerate(refs[:-1]):
        x = ref[...].astype(jnp.float32)
        square = x * x
        high = square.astype(jnp.bfloat16)
        low = (square - high.astype(jnp.float32)).astype(jnp.bfloat16)
        total = lax.dot_general(ones, high, contract, preferred_element_type=jnp.float32)
        total = total + lax.dot_general(ones, low, contract, preferred_element_type=jnp.float32)
        out_ref[i:i + 1, :] = total[0:1, :]


def square_call(parts):
    return pl.pallas_call(
        square_kernel,
        out_shape=jax.ShapeDtypeStruct((len(parts), FT), jnp.float32),
        compiler_params=pltpu.CompilerParams(vmem_limit_bytes=32 * 1024 * 1024),
        name="row_squares",
        cost_estimate=pl.CostEstimate(flops=10**9, bytes_accessed=4 * 10**6, transcendentals=0),
    )(*parts)


def head_call(bias, keys, values, query, grad):
    vm = pltpu.VMEM
    bf, f32 = jnp.bfloat16, jnp.float32
    width = query.shape[1]
    rows = pl.BlockSpec((FT, BLK), lambda i: (0, i))
    return pl.pallas_call(
        head_kernel,
        grid=(width // BLK,),
        in_specs=[
            pl.BlockSpec((4 * SLOTS, FT), lambda i: (0, 0)),
        ]
        + [rows] * (2 * SLOTS + 2),
        out_specs=[rows] * (2 + 2 * SLOTS),
        out_shape=[jax.ShapeDtypeStruct((FT, width), bf), jax.ShapeDtypeStruct((FT, width), f32)]
        + [jax.ShapeDtypeStruct((FT, width), bf)] * (2 * SLOTS),
        scratch_shapes=[
            vm((KEYS, BLK), bf),
            vm((KEYS, BLK), bf),
            vm((KEYS, FT), f32),
        ],
        compiler_params=pltpu.CompilerParams(vmem_limit_bytes=56 * 1024 * 1024),
        name="head_attention",
        cost_estimate=pl.CostEstimate(flops=9 * 10**9, bytes_accessed=12 * 10**6, transcendentals=12 * 10**6),
    )(bias, *keys, *values, query, grad)


epsilon = 1e-06


def across(value, late):
    count = lax.axis_size("tm")
    pairs = [(s, s ^ 2) if not late else (s, ((s + 2) ^ 2) - 2) for s in range(count)]
    return lax.ppermute(value, "tm", [(a, b) for a, b in pairs if 0 <= b < count])


def ring_sum(value):
    rounds = ((1, 0, 3, 2, 5, 4, 7, 6), (7, 2, 1, 4, 3, 6, 5, 0), (3, 6, 5, 0, 7, 2, 1, 4))
    for partners in rounds:
        value = value + lax.ppermute(value, "head", list(enumerate(partners)))
    return value


def swapped(value):
    return lax.ppermute(value, "tm", [(s, s ^ 1) for s in range(lax.axis_size("tm"))])


def outward(value):
    count = lax.axis_size("tm")
    pairs = [(s, s + 1) if s % 2 else (s, s - 1) for s in range(count)]
    return lax.ppermute(value, "tm", [(a, b) for a, b in pairs if 0 <= b < count])


def band(value, cross):
    early, late = across(value, False), across(value, True)
    beside = swapped(value)
    outer = outward(jnp.where(cross, early, late))
    return [value, early, late, beside, swapped(early), swapped(late), outer]


def paired(terms, cross):
    f32 = jnp.float32
    outer = outward(terms[6]).astype(f32)
    early = terms[1].astype(f32) + swapped(terms[4]).astype(f32) + jnp.where(cross, outer, 0.0)
    late = terms[2].astype(f32) + swapped(terms[5]).astype(f32) + jnp.where(cross, 0.0, outer)
    return early.astype(jnp.bfloat16), late.astype(jnp.bfloat16)


def returned(terms, early, late):
    return [terms[0], swapped(terms[3]), across(early, False), across(late, True)]


def summed(parts):
    total = parts[0].astype(jnp.float32)
    for part in parts[1:]:
        total = total + part.astype(jnp.float32)
    return total


def local(queries, key_rows, value_rows, query_gain, key_gain, block_mask, out_grad):
    frame = lax.axis_index("tm")
    frame_count = lax.axis_size("tm")
    core = 1 - 2 * (frame % 2)
    chip = 2 - 4 * (frame // 2 % 2)
    cross = core * chip > 0
    full_width = queries.shape[1] * lax.axis_size("head")
    values = band(value_rows, cross)

    offsets = jnp.stack([0 * core, chip, -chip, core, core + chip, core - chip, -3 * core])
    mask_rows = lax.dynamic_index_in_dim(block_mask, frame, 0, keepdims=False)
    is_valid = (frame + offsets >= 0) & (frame + offsets < frame_count)
    live = jnp.where(is_valid[:, None, None], mask_rows[offsets + 3], 0)
    bias = jnp.where(jnp.swapaxes(live, 1, 2) > 0, 0.0, NEG).reshape(SLOTS * live.shape[2], live.shape[1])
    bias = jnp.repeat(bias, BLK, axis=1)

    query_float = queries.astype(jnp.float32)
    key_float = key_rows.astype(jnp.float32)
    key_raw, values[3] = lax.optimization_barrier((key_rows, values[3]))
    rates = lax.rsqrt(ring_sum(square_call([queries, key_raw])) / full_width + epsilon)
    query_rate = rates[0][:, None]
    key_rate = rates[1][:, None]
    query_scaled = (query_float * query_rate * query_gain * (SCALE * LOG2E)).astype(jnp.bfloat16)
    keys = band((key_float * key_rate * key_gain).astype(jnp.bfloat16), cross)

    out = head_call(bias, keys, values, query_scaled, out_grad)
    attended, grad_qnorm = out[:2]
    key_terms, value_terms = out[2:2 + SLOTS], out[2 + SLOTS:]
    key_parts = returned(key_terms, *paired(key_terms, cross))
    value_near = paired(value_terms, cross)
    key_parts, value_near = lax.optimization_barrier((key_parts, value_near))
    value_parts = returned(value_terms, *value_near)
    grad_knorm = summed(key_parts)
    dots = jnp.stack(
        [
            jnp.sum(query_float * query_gain * grad_qnorm, axis=1),
            jnp.sum(key_float * key_gain * grad_knorm, axis=1),
        ]
    )
    dots, value_parts = lax.optimization_barrier((ring_sum(dots), value_parts))
    query_dot, key_dot = dots
    value_sum = summed(value_parts)
    query_grad = (
        query_rate * query_gain * grad_qnorm
        - query_float * query_rate**3 * query_dot[:, None] / full_width
    )
    key_grad = (
        key_rate * key_gain * grad_knorm - key_float * key_rate**3 * key_dot[:, None] / full_width
    )
    return (
        attended,
        query_grad.astype(jnp.bfloat16),
        key_grad.astype(jnp.bfloat16),
        value_sum.astype(jnp.bfloat16),
    )


def solution(mesh):
    return jax.shard_map(
        local,
        mesh=mesh,
        in_specs=(
            P("tm", "head"),
            P("tm", "head"),
            P("tm", "head"),
            P("head"),
            P("head"),
            P(),
            P("tm", "head"),
        ),
        out_specs=(P("tm", "head"), P("tm", "head"), P("tm", "head"), P("tm", "head")),
        check_vma=False,
    )
```

```python
import functools
import jax, jax.numpy as jnp
from jax import lax
from jax.sharding import PartitionSpec as P
from jax.experimental import pallas as pl
from jax.experimental.pallas import tpu as pltpu

LOG2E = 1.4426950408889634
LN2 = 0.6931471805599453
SCALE = 128 ** -0.5
NEG = -1e30
BLK = 128
FT = 512
SLOTS = 7
KEYS = SLOTS * FT


def head_kernel(bias_ref, *refs):
    key_refs = refs[:SLOTS]
    value_refs = refs[SLOTS:2 * SLOTS]
    q_ref, g_ref, att_ref, gq_ref = refs[2 * SLOTS:2 * SLOTS + 4]
    term_refs = refs[2 * SLOTS + 4:4 * SLOTS + 4]
    kb, vb, st = refs[4 * SLOTS + 4:]
    f32, bf = jnp.float32, jnp.bfloat16
    q = q_ref[...]
    g = g_ref[...]
    qt = q.T
    gt = g.T

    def fold(x, op):
        return op(x.reshape(-1, 8, FT), axis=0)

    m8 = jnp.full((8, FT), NEG, f32)
    for s in range(SLOTS):
        cols = slice(s * FT, (s + 1) * FT)
        kb[cols, :] = key_refs[s][...]
        vb[cols, :] = value_refs[s][...]
    for lo, hi in [(0, 2), (2, 4), (4, 6), (6, 7)]:
        cols = slice(lo * FT, hi * FT)
        x = jnp.dot(kb[cols, :], qt, preferred_element_type=f32)
        for b in range(4 * (hi - lo)):
            y = x[b * BLK:(b + 1) * BLK] + bias_ref[4 * lo + b:4 * lo + b + 1, :]
            st[lo * FT + b * BLK:lo * FT + (b + 1) * BLK, :] = y
            m8 = jnp.maximum(m8, fold(y, jnp.max))
    top = jnp.max(m8, axis=0, keepdims=True)

    l8 = jnp.zeros((8, FT), f32)
    ot = jnp.zeros((BLK, FT), f32)
    for lo, hi in [(0, 2), (2, 4), (4, 6), (6, 7)]:
        cols = slice(lo * FT, hi * FT)
        e = jnp.exp2(st[cols, :] - top)
        l8 = l8 + fold(e, jnp.sum)
        ot = ot + lax.dot_general(vb[cols, :], e.astype(bf), (((0,), (0,)), ((), ())), preferred_element_type=f32)
    total = jnp.sum(l8, axis=0, keepdims=True)
    lse = top + jnp.log2(total)
    att = (ot / total).astype(bf)
    delta = jnp.sum(gt.astype(f32) * att.astype(f32), axis=0, keepdims=True)
    att_ref[...] = att.T

    dqt = jnp.zeros((BLK, FT), f32)
    for lo, hi in [(0, 2), (2, 4), (4, 6), (6, 7)]:
        cols = slice(lo * FT, hi * FT)
        w = jnp.exp2(st[cols, :] - lse)
        gw = jnp.dot(vb[cols, :], gt, preferred_element_type=f32)
        ds = (w * (gw - delta)).astype(bf)
        dqt = dqt + lax.dot_general(kb[cols, :], ds, (((0,), (0,)), ((), ())), preferred_element_type=f32)
        dk = (jnp.dot(ds, q, preferred_element_type=f32) * LN2).astype(bf)
        dv = jnp.dot(w.astype(bf), g, preferred_element_type=f32).astype(bf)
        for s in range(lo, hi):
            part = slice((s - lo) * FT, (s - lo + 1) * FT)
            term_refs[s][...] = dk[part]
            term_refs[SLOTS + s][...] = dv[part]
    gq_ref[...] = dqt.T * SCALE


def square_kernel(*refs):
    out_ref = refs[-1]
    ones = jnp.ones((8, refs[0].shape[1]), jnp.bfloat16)
    contract = (((1,), (1,)), ((), ()))
    for i, ref in enumerate(refs[:-1]):
        x = ref[...].astype(jnp.float32)
        square = x * x
        high = square.astype(jnp.bfloat16)
        low = (square - high.astype(jnp.float32)).astype(jnp.bfloat16)
        total = lax.dot_general(ones, high, contract, preferred_element_type=jnp.float32)
        total = total + lax.dot_general(ones, low, contract, preferred_element_type=jnp.float32)
        out_ref[i:i + 1, :] = total[0:1, :]


def square_call(parts):
    return pl.pallas_call(
        square_kernel,
        out_shape=jax.ShapeDtypeStruct((len(parts), FT), jnp.float32),
        compiler_params=pltpu.CompilerParams(vmem_limit_bytes=32 * 1024 * 1024),
        name="row_squares",
        cost_estimate=pl.CostEstimate(flops=10**9, bytes_accessed=4 * 10**6, transcendentals=0),
    )(*parts)


def head_call(bias, keys, values, query, grad):
    vm = pltpu.VMEM
    bf, f32 = jnp.bfloat16, jnp.float32
    width = query.shape[1]
    rows = pl.BlockSpec((FT, BLK), lambda i: (0, i))
    return pl.pallas_call(
        head_kernel,
        grid=(width // BLK,),
        in_specs=[
            pl.BlockSpec((4 * SLOTS, FT), lambda i: (0, 0)),
        ]
        + [rows] * (2 * SLOTS + 2),
        out_specs=[rows] * (2 + 2 * SLOTS),
        out_shape=[jax.ShapeDtypeStruct((FT, width), bf), jax.ShapeDtypeStruct((FT, width), f32)]
        + [jax.ShapeDtypeStruct((FT, width), bf)] * (2 * SLOTS),
        scratch_shapes=[
            vm((KEYS, BLK), bf),
            vm((KEYS, BLK), bf),
            vm((KEYS, FT), f32),
        ],
        compiler_params=pltpu.CompilerParams(vmem_limit_bytes=56 * 1024 * 1024),
        name="head_attention",
        cost_estimate=pl.CostEstimate(flops=9 * 10**9, bytes_accessed=12 * 10**6, transcendentals=12 * 10**6),
    )(bias, *keys, *values, query, grad)


epsilon = 1e-06


def across(value, late):
    count = lax.axis_size("tm")
    pairs = [(s, s ^ 2) if not late else (s, ((s + 2) ^ 2) - 2) for s in range(count)]
    return lax.ppermute(value, "tm", [(a, b) for a, b in pairs if 0 <= b < count])


def turned(value, steps):
    count = lax.axis_size("head")
    return lax.ppermute(value, "head", [(s, (s + steps) % count) for s in range(count)])


def ring_sum(value):
    after, before = turned(value, -1), turned(value, 1)
    pair = value + after
    return pair + before + turned(pair + before, -3) + turned(pair, 3)


def pair_sum(value):
    rounds = ((1, 0, 3, 2, 5, 4, 7, 6), (7, 2, 1, 4, 3, 6, 5, 0), (3, 6, 5, 0, 7, 2, 1, 4))
    for partners in rounds:
        value = value + lax.ppermute(value, "head", list(enumerate(partners)))
    return value


def swapped(value):
    return lax.ppermute(value, "tm", [(s, s ^ 1) for s in range(lax.axis_size("tm"))])


def outward(value):
    count = lax.axis_size("tm")
    pairs = [(s, s + 1) if s % 2 else (s, s - 1) for s in range(count)]
    return lax.ppermute(value, "tm", [(a, b) for a, b in pairs if 0 <= b < count])


def band(value, cross):
    early, late = across(value, False), across(value, True)
    beside = swapped(value)
    outer = outward(jnp.where(cross, early, late))
    return [value, early, late, beside, swapped(early), swapped(late), outer]


def paired(terms, cross):
    f32 = jnp.float32
    outer = outward(terms[6]).astype(f32)
    early = terms[1].astype(f32) + swapped(terms[4]).astype(f32) + jnp.where(cross, outer, 0.0)
    late = terms[2].astype(f32) + swapped(terms[5]).astype(f32) + jnp.where(cross, 0.0, outer)
    return early.astype(jnp.bfloat16), late.astype(jnp.bfloat16)


def returned(terms, early, late):
    return [terms[0], swapped(terms[3]), across(early, False), across(late, True)]


def summed(parts):
    total = parts[0].astype(jnp.float32)
    for part in parts[1:]:
        total = total + part.astype(jnp.float32)
    return total


def local(queries, key_rows, value_rows, query_gain, key_gain, block_mask, out_grad):
    frame = lax.axis_index("tm")
    frame_count = lax.axis_size("tm")
    core = 1 - 2 * (frame % 2)
    chip = 2 - 4 * (frame // 2 % 2)
    cross = core * chip > 0
    full_width = queries.shape[1] * lax.axis_size("head")
    values = band(value_rows, cross)

    offsets = jnp.stack([0 * core, chip, -chip, core, core + chip, core - chip, -3 * core])
    mask_rows = lax.dynamic_index_in_dim(block_mask, frame, 0, keepdims=False)
    is_valid = (frame + offsets >= 0) & (frame + offsets < frame_count)
    live = jnp.where(is_valid[:, None, None], mask_rows[offsets + 3], 0)
    bias = jnp.where(jnp.swapaxes(live, 1, 2) > 0, 0.0, NEG).reshape(SLOTS * live.shape[2], live.shape[1])
    bias = jnp.repeat(bias, BLK, axis=1)

    query_float = queries.astype(jnp.float32)
    key_float = key_rows.astype(jnp.float32)
    key_raw, values[3] = lax.optimization_barrier((key_rows, values[3]))
    rates = lax.rsqrt(pair_sum(square_call([queries, key_raw])) / full_width + epsilon)
    query_rate = rates[0][:, None]
    key_rate = rates[1][:, None]
    query_scaled = (query_float * query_rate * query_gain * (SCALE * LOG2E)).astype(jnp.bfloat16)
    keys = band((key_float * key_rate * key_gain).astype(jnp.bfloat16), cross)

    out = head_call(bias, keys, values, query_scaled, out_grad)
    attended, grad_qnorm = out[:2]
    key_terms, value_terms = out[2:2 + SLOTS], out[2 + SLOTS:]
    key_parts = returned(key_terms, *paired(key_terms, cross))
    value_near = paired(value_terms, cross)
    key_parts, value_near = lax.optimization_barrier((key_parts, value_near))
    value_parts = returned(value_terms, *value_near)
    grad_knorm = summed(key_parts)
    dots = jnp.stack(
        [
            jnp.sum(query_float * query_gain * grad_qnorm, axis=1),
            jnp.sum(key_float * key_gain * grad_knorm, axis=1),
        ]
    )
    dots, value_parts = lax.optimization_barrier((ring_sum(dots), value_parts))
    query_dot, key_dot = dots
    value_sum = summed(value_parts)
    query_grad = (
        query_rate * query_gain * grad_qnorm
        - query_float * query_rate**3 * query_dot[:, None] / full_width
    )
    key_grad = (
        key_rate * key_gain * grad_knorm - key_float * key_rate**3 * key_dot[:, None] / full_width
    )
    return (
        attended,
        query_grad.astype(jnp.bfloat16),
        key_grad.astype(jnp.bfloat16),
        value_sum.astype(jnp.bfloat16),
    )


def solution(mesh):
    return jax.shard_map(
        local,
        mesh=mesh,
        in_specs=(
            P("tm", "head"),
            P("tm", "head"),
            P("tm", "head"),
            P("head"),
            P("head"),
            P(),
            P("tm", "head"),
        ),
        out_specs=(P("tm", "head"), P("tm", "head"), P("tm", "head"), P("tm", "head")),
        check_vma=False,
    )
```

```python
import functools
import jax, jax.numpy as jnp
from jax import lax
from jax.sharding import PartitionSpec as P
from jax.experimental import pallas as pl
from jax.experimental.pallas import tpu as pltpu

LOG2E = 1.4426950408889634
LN2 = 0.6931471805599453
SCALE = 128 ** -0.5
NEG = -1e30
BLK = 128
FT = 512
SLOTS = 7
KEYS = SLOTS * FT


def head_kernel(bias_ref, *refs):
    key_refs = refs[:SLOTS]
    value_refs = refs[SLOTS:2 * SLOTS]
    q_ref, g_ref, att_ref, gq_ref = refs[2 * SLOTS:2 * SLOTS + 4]
    term_refs = refs[2 * SLOTS + 4:4 * SLOTS + 4]
    kb, vb, st = refs[4 * SLOTS + 4:]
    f32, bf = jnp.float32, jnp.bfloat16
    q = q_ref[...]
    g = g_ref[...]
    qt = q.T
    gt = g.T

    def fold(x, op):
        return op(x.reshape(-1, 8, FT), axis=0)

    m8 = jnp.full((8, FT), NEG, f32)
    for s in range(SLOTS):
        cols = slice(s * FT, (s + 1) * FT)
        kb[cols, :] = key_refs[s][...]
        vb[cols, :] = value_refs[s][...]
    for lo, hi in [(0, 2), (2, 4), (4, 6), (6, 7)]:
        cols = slice(lo * FT, hi * FT)
        x = jnp.dot(kb[cols, :], qt, preferred_element_type=f32)
        for b in range(4 * (hi - lo)):
            y = x[b * BLK:(b + 1) * BLK] + bias_ref[4 * lo + b:4 * lo + b + 1, :]
            st[lo * FT + b * BLK:lo * FT + (b + 1) * BLK, :] = y
            m8 = jnp.maximum(m8, fold(y, jnp.max))
    top = jnp.max(m8, axis=0, keepdims=True)

    l8 = jnp.zeros((8, FT), f32)
    ot = jnp.zeros((BLK, FT), f32)
    for lo, hi in [(0, 2), (2, 4), (4, 6), (6, 7)]:
        cols = slice(lo * FT, hi * FT)
        e = jnp.exp2(st[cols, :] - top)
        l8 = l8 + fold(e, jnp.sum)
        ot = ot + lax.dot_general(vb[cols, :], e.astype(bf), (((0,), (0,)), ((), ())), preferred_element_type=f32)
    total = jnp.sum(l8, axis=0, keepdims=True)
    lse = top + jnp.log2(total)
    att = (ot / total).astype(bf)
    delta = jnp.sum(gt.astype(f32) * att.astype(f32), axis=0, keepdims=True)
    att_ref[...] = att.T

    dqt = jnp.zeros((BLK, FT), f32)
    for lo, hi in [(0, 2), (2, 4), (4, 6), (6, 7)]:
        cols = slice(lo * FT, hi * FT)
        w = jnp.exp2(st[cols, :] - lse)
        gw = jnp.dot(vb[cols, :], gt, preferred_element_type=f32)
        ds = (w * (gw - delta)).astype(bf)
        dqt = dqt + lax.dot_general(kb[cols, :], ds, (((0,), (0,)), ((), ())), preferred_element_type=f32)
        dk = (jnp.dot(ds, q, preferred_element_type=f32) * LN2).astype(bf)
        dv = jnp.dot(w.astype(bf), g, preferred_element_type=f32).astype(bf)
        for s in range(lo, hi):
            part = slice((s - lo) * FT, (s - lo + 1) * FT)
            term_refs[s][...] = dk[part]
            term_refs[SLOTS + s][...] = dv[part]
    gq_ref[...] = dqt.T * SCALE


def square_kernel(*refs):
    out_ref = refs[-1]
    ones = jnp.ones((8, refs[0].shape[1]), jnp.bfloat16)
    contract = (((1,), (1,)), ((), ()))
    for i, ref in enumerate(refs[:-1]):
        x = ref[...].astype(jnp.float32)
        square = x * x
        high = square.astype(jnp.bfloat16)
        low = (square - high.astype(jnp.float32)).astype(jnp.bfloat16)
        total = lax.dot_general(ones, high, contract, preferred_element_type=jnp.float32)
        total = total + lax.dot_general(ones, low, contract, preferred_element_type=jnp.float32)
        out_ref[i:i + 1, :] = total[0:1, :]


def square_call(parts):
    return pl.pallas_call(
        square_kernel,
        out_shape=jax.ShapeDtypeStruct((len(parts), FT), jnp.float32),
        compiler_params=pltpu.CompilerParams(vmem_limit_bytes=32 * 1024 * 1024),
        name="row_squares",
        cost_estimate=pl.CostEstimate(flops=10**9, bytes_accessed=4 * 10**6, transcendentals=0),
    )(*parts)


def head_call(bias, keys, values, query, grad):
    vm = pltpu.VMEM
    bf, f32 = jnp.bfloat16, jnp.float32
    width = query.shape[1]
    rows = pl.BlockSpec((FT, BLK), lambda i: (0, i))
    return pl.pallas_call(
        head_kernel,
        grid=(width // BLK,),
        in_specs=[
            pl.BlockSpec((4 * SLOTS, FT), lambda i: (0, 0)),
        ]
        + [rows] * (2 * SLOTS + 2),
        out_specs=[rows] * (2 + 2 * SLOTS),
        out_shape=[jax.ShapeDtypeStruct((FT, width), bf), jax.ShapeDtypeStruct((FT, width), f32)]
        + [jax.ShapeDtypeStruct((FT, width), bf)] * (2 * SLOTS),
        scratch_shapes=[
            vm((KEYS, BLK), bf),
            vm((KEYS, BLK), bf),
            vm((KEYS, FT), f32),
        ],
        compiler_params=pltpu.CompilerParams(vmem_limit_bytes=56 * 1024 * 1024),
        name="head_attention",
        cost_estimate=pl.CostEstimate(flops=9 * 10**9, bytes_accessed=12 * 10**6, transcendentals=12 * 10**6),
    )(bias, *keys, *values, query, grad)


epsilon = 1e-06


def across(value, late):
    count = lax.axis_size("tm")
    pairs = [(s, s ^ 2) if not late else (s, ((s + 2) ^ 2) - 2) for s in range(count)]
    return lax.ppermute(value, "tm", [(a, b) for a, b in pairs if 0 <= b < count])


def turned(value, steps):
    count = lax.axis_size("head")
    return lax.ppermute(value, "head", [(s, (s + steps) % count) for s in range(count)])


def ring_sum(value):
    after, before = turned(value, -1), turned(value, 1)
    pair = value + after
    return pair + before + turned(pair + before, -3) + turned(pair, 3)


def pair_sum(value):
    rounds = ((1, 0, 3, 2, 5, 4, 7, 6), (7, 2, 1, 4, 3, 6, 5, 0), (3, 6, 5, 0, 7, 2, 1, 4))
    for partners in rounds:
        value = value + lax.ppermute(value, "head", list(enumerate(partners)))
    return value


def swapped(value):
    return lax.ppermute(value, "tm", [(s, s ^ 1) for s in range(lax.axis_size("tm"))])


def outward(value):
    count = lax.axis_size("tm")
    pairs = [(s, s + 1) if s % 2 else (s, s - 1) for s in range(count)]
    return lax.ppermute(value, "tm", [(a, b) for a, b in pairs if 0 <= b < count])


def band(value, cross):
    early, late = across(value, False), across(value, True)
    beside = swapped(value)
    outer = outward(jnp.where(cross, early, late))
    return [value, early, late, beside, swapped(early), swapped(late), outer]


def paired(terms, cross):
    f32 = jnp.float32
    outer = outward(terms[6]).astype(f32)
    early = terms[1].astype(f32) + swapped(terms[4]).astype(f32) + jnp.where(cross, outer, 0.0)
    late = terms[2].astype(f32) + swapped(terms[5]).astype(f32) + jnp.where(cross, 0.0, outer)
    return early.astype(jnp.bfloat16), late.astype(jnp.bfloat16)


def returned(terms, early, late):
    return [terms[0], swapped(terms[3]), across(early, False), across(late, True)]


def summed(parts):
    total = parts[0].astype(jnp.float32)
    for part in parts[1:]:
        total = total + part.astype(jnp.float32)
    return total


def local(queries, key_rows, value_rows, query_gain, key_gain, block_mask, out_grad):
    frame = lax.axis_index("tm")
    frame_count = lax.axis_size("tm")
    core = 1 - 2 * (frame % 2)
    chip = 2 - 4 * (frame // 2 % 2)
    cross = core * chip > 0
    full_width = queries.shape[1] * lax.axis_size("head")
    values = band(value_rows, cross)

    offsets = jnp.stack([0 * core, chip, -chip, core, core + chip, core - chip, -3 * core])
    mask_rows = lax.dynamic_index_in_dim(block_mask, frame, 0, keepdims=False)
    is_valid = (frame + offsets >= 0) & (frame + offsets < frame_count)
    live = jnp.where(is_valid[:, None, None], mask_rows[offsets + 3], 0)
    bias = jnp.where(jnp.swapaxes(live, 1, 2) > 0, 0.0, NEG).reshape(SLOTS * live.shape[2], live.shape[1])
    bias = jnp.repeat(bias, BLK, axis=1)

    query_float = queries.astype(jnp.float32)
    key_float = key_rows.astype(jnp.float32)
    key_raw, values[3] = lax.optimization_barrier((key_rows, values[3]))
    rates = lax.rsqrt(pair_sum(square_call([queries, key_raw])) / full_width + epsilon)
    query_rate = rates[0][:, None]
    key_rate = rates[1][:, None]
    query_scaled = (query_float * query_rate * query_gain * (SCALE * LOG2E)).astype(jnp.bfloat16)
    keys = band((key_float * key_rate * key_gain).astype(jnp.bfloat16), cross)

    out = head_call(bias, keys, values, query_scaled, out_grad)
    attended, grad_qnorm = out[:2]
    key_terms, value_terms = out[2:2 + SLOTS], out[2 + SLOTS:]
    key_parts = returned(key_terms, *paired(key_terms, cross))
    value_near = paired(value_terms, cross)
    key_parts, value_near = lax.optimization_barrier((key_parts, value_near))
    value_parts = returned(value_terms, *value_near)
    grad_knorm = summed(key_parts)
    dots = jnp.stack(
        [
            jnp.sum(query_float * query_gain * grad_qnorm, axis=1),
            jnp.sum(key_float * key_gain * grad_knorm, axis=1),
        ]
    )
    query_dot, key_dot = ring_sum(dots)
    query_grad = (
        query_rate * query_gain * grad_qnorm
        - query_float * query_rate**3 * query_dot[:, None] / full_width
    )
    key_grad = (
        key_rate * key_gain * grad_knorm - key_float * key_rate**3 * key_dot[:, None] / full_width
    )
    query_grad, key_grad = query_grad.astype(jnp.bfloat16), key_grad.astype(jnp.bfloat16)
    query_grad, key_grad, value_parts = lax.optimization_barrier((query_grad, key_grad, value_parts))
    return attended, query_grad, key_grad, summed(value_parts).astype(jnp.bfloat16)


def solution(mesh):
    return jax.shard_map(
        local,
        mesh=mesh,
        in_specs=(
            P("tm", "head"),
            P("tm", "head"),
            P("tm", "head"),
            P("head"),
            P("head"),
            P(),
            P("tm", "head"),
        ),
        out_specs=(P("tm", "head"), P("tm", "head"), P("tm", "head"), P("tm", "head")),
        check_vma=False,
    )
```
